32 devices in a mesh: dp: 4 (over y, core), expert: 8 (over z, x).
Axes of the slice: x: 2, y: 2, z: 4, core: 2. Of those that a mesh axis runs over, the one named last changes fastest.
Arguments:
- tokens: bfloat16 [4096, 2048], P(('dp', 'expert')), may hold values from -6 to 6
- cotangent: bfloat16 [4096, 2048], P(('dp', 'expert')), may hold values from -6 to 6
- hot_mask: int32 [4096], P(('dp', 'expert')), may hold values 0 or 1
- hot_gate: float32 [4096], P(('dp', 'expert')), may hold values from 0.2 to 1
- cold_ids: int32 [4096, 1], P(('dp', 'expert')), may hold values from 0 to 3; in each aligned block of 128 rows (0 to 127, 128 to 255, ...) at most 40 rows name the same one
- cold_gate: float32 [4096, 1], P(('dp', 'expert')), may hold values from 0.2 to 1
- hot_in: bfloat16 [2, 704, 2048], P(None, 'dp'), may hold values from -0.125 to 0.125
- hot_down: bfloat16 [704, 2048], P('dp'), may hold values from -0.21875 to 0.21875
- cold_in: bfloat16 [2, 2816, 2048], P(None, 'expert'), may hold values from -0.125 to 0.125
- cold_down: bfloat16 [2816, 2048], P('expert'), may hold values from -0.21875 to 0.21875
Outputs:
- mixed: bfloat16 [4096, 2048], P(('dp', 'expert'))
- input_grad: bfloat16 [4096, 2048], P(('dp', 'expert'))
- hot_grad_in: float32 [2, 704, 2048], P(None, 'dp', 'expert')
- hot_grad_down: float32 [704, 2048], P('dp', 'expert')
- cold_grad_in: bfloat16 [4, 2, 2816, 2048], P('dp', None, 'expert')
- cold_grad_down: bfloat16 [4, 2816, 2048], P('dp', 'expert')
The draws below stay inside these ranges and needn't reach their ends.
Inputs may be any that keep to these rules, and one draw needn't show every extreme that they name: `cold_ids`: in each device's block of 128 rows no cold expert is chosen by more than 40 rows, and in every draw some device's block chooses some cold expert exactly 40 times.
All inputs are finite; a program needn't handle non-finite values. No bound on the sum of `hot_mask` on one device may be relied on, other than what follows from the above.
Results may differ from the reference program's by a relative error of at most 0.0059.
Values may be sent and summed in bfloat16 or wider, within the bound.
A program may use at most 128 MiB of HBM per device.

```python
import math
import jax
import jax.numpy as jnp
import numpy as np
from jax import lax

D = 2048
FFW = 704
TOPC = 1
TOK_DEV = 128
COLD = 4
CAP = 40
TOKENS = 4096
N_DP = 4
N_EXPERT = 8


def plant(array, stream_key, low, top_value):
    extent = array.shape
    index_at = [jax.random.randint(jax.random.fold_in(stream_key, axis), (), 0, extent[axis]) for axis in range(len(extent))]
    array = array.at[tuple(index_at)].set(low)
    longest = extent.index(max(extent))
    index_at[longest] = (index_at[longest] + 1) % extent[longest]
    return array.at[tuple(index_at)].set(top_value)


def block_scale(key, extent, shards, low, high):
    loudness, own = 1.0, jax.random.fold_in(key, 6)
    for position, parts in shards:
        steps = jnp.exp(jax.random.uniform(jax.random.fold_in(own, position), (parts,), jnp.float32, low / len(shards), high / len(shards)))
        loudness = loudness * jnp.repeat(steps, extent[position] // parts).reshape([-1 if axis == position else 1 for axis in range(len(extent))])
    return loudness


def assign_block(stream_key, own, number, rows, number_of, top, bound, slope):
    order = jax.random.permutation(stream_key, number_of)
    crowded, ordinary = shares(number_of, rows * top, bound, slope, True), shares(number_of, rows * top, bound, slope, False)
    places = jnp.arange(number_of)

    def named(lengths, offset_by):
        used = int((lengths > 0).sum())
        fixed = max(1, used // 4)
        passed = fixed + (places - fixed + offset_by * (used - fixed)) % max(1, number_of - fixed)
        return jnp.zeros((number_of,), jnp.int32).at[order[jnp.where(places < fixed, places, passed)]].set(jnp.asarray(lengths, jnp.int32))

    lengths = jnp.where(number % 4 == 0, named(crowded, number // 4), named(ordinary, number - number // 4 - 1))
    mixed = jax.random.permutation(jax.random.fold_in(own, 3), number_of)
    giver, sink = mixed[0:number_of // 2 * 2:2], mixed[1:number_of // 2 * 2:2]
    room = jnp.minimum(lengths[giver] - 1, bound - lengths[sink]) // 2
    room = jnp.where((giver == order[0]) | (sink == order[0]) | (lengths[sink] == 0), 0, jnp.maximum(room, 0))
    passed = jax.random.randint(jax.random.fold_in(own, 4), (number_of // 2,), 0, 1 << 20) % (room + 1)
    lengths = lengths.at[giver].add(-passed).at[sink].add(passed)
    members = jnp.searchsorted(jnp.cumsum(lengths), jnp.arange(rows * top), side="right").astype(jnp.int32)
    grid = members.reshape(top, rows).T
    grid = grid[jax.random.permutation(jax.random.fold_in(own, 1), rows)]
    offset_by = jax.random.randint(jax.random.fold_in(own, 2), (rows, 1), 0, top)
    return jnp.take_along_axis(grid, (jnp.arange(top)[None, :] + offset_by) % top, axis=1)


def shares(number_of, total, limit, slope, full):
    weights = [(1 << 20) // math.isqrt(grade ** slope) + 1 for grade in range(1, number_of + 1)]
    largest = limit if full else min(limit, max(-(-total // number_of), total * weights[0] // sum(weights)))
    least = 1 if total - largest >= number_of - 1 else 0
    counts, rest = [largest] + [least] * (number_of - 1), total - largest - least * (number_of - 1)
    while rest > 0:
        movable = [i for i in range(1, number_of) if counts[i] < largest] or [i for i in range(1, number_of) if counts[i] < limit]
        mass, left = sum([weights[i] for i in movable]), rest
        for i in movable:
            addition = min(limit - counts[i], max(1, left * weights[i] // mass), rest)
            counts[i] = counts[i] + addition
            rest = rest - addition
    return np.array(counts)


def centred(own_key, dims, deviation, bound, split=(), kind=jnp.bfloat16):
    values = deviation * jax.random.normal(own_key, dims, jnp.float32)
    if split:
        values = values * block_scale(own_key, dims, split, -0.22, 0.18)
    return jnp.clip(values, -bound, bound).astype(kind)


def setup_inputs(seed: int = 0) -> dict:
    key_of = jax.random.split(jax.random.key(seed), 11)
    tokens = centred(key_of[0], (TOKENS, D), 1.0, 6.0, ((0, 32),))
    cotangent = centred(key_of[1], (TOKENS, D), 1.0, 6.0, ((0, 32),))
    hot_mask = plant((jax.random.randint(key_of[2], (TOKENS,), 0, 4) < 3).astype(jnp.int32), jax.random.fold_in(key_of[2], 1), 0, 1)
    hot_gate = jnp.clip(0.2 + 0.8 * jax.random.uniform(key_of[3], (TOKENS,), jnp.float32) ** block_scale(key_of[3], (TOKENS,), ((0, 32),), -0.2, 0.2), 0.2, 1.0)
    cold_ids_keys = jax.random.split(jax.random.fold_in(key_of[4], 1), TOKENS // TOK_DEV)
    cold_ids_turns = jax.random.permutation(jax.random.fold_in(key_of[4], 3), TOKENS // TOK_DEV)
    cold_ids = jax.vmap(lambda own, number: assign_block(jax.random.fold_in(key_of[4], 2), own, number, TOK_DEV, COLD, TOPC, CAP, 2))(cold_ids_keys, cold_ids_turns).reshape((TOKENS, TOPC))
    cold_gate = jnp.clip(0.2 + 0.8 * jax.random.uniform(key_of[5], (TOKENS, TOPC), jnp.float32) ** block_scale(key_of[5], (TOKENS, TOPC), ((0, 32),), -0.2, 0.2), 0.2, 1.0)
    hot_in = centred(key_of[6], (2, FFW, D), D ** -0.5, 0.125, ((1, 4),))
    hot_down = centred(key_of[7], (FFW, D), FFW ** -0.5, 0.21875, ((0, 4),))
    cold_in = centred(key_of[8], (2, COLD * FFW, D), D ** -0.5, 0.125, ((1, 8),))
    cold_down = centred(key_of[9], (COLD * FFW, D), FFW ** -0.5, 0.21875, ((0, 8),))
    return dict(tokens=tokens, cotangent=cotangent, hot_mask=hot_mask, hot_gate=hot_gate, cold_ids=cold_ids, cold_gate=cold_gate, hot_in=hot_in, hot_down=hot_down, cold_in=cold_in, cold_down=cold_down)


def silu_parts(values):
    sigmoid_val = jax.nn.sigmoid(values)
    return (values * sigmoid_val, sigmoid_val * (1.0 + values * (1.0 - sigmoid_val)))

def reference(tokens, cotangent, hot_mask, hot_gate, cold_ids, cold_gate, hot_in, hot_down, cold_in, cold_down):
    hot_weight = hot_mask.astype(jnp.float32) * hot_gate
    gate_pre = jnp.dot(tokens, hot_in[0].T, preferred_element_type=jnp.float32)
    up_pre = jnp.dot(tokens, hot_in[1].T, preferred_element_type=jnp.float32)
    silu_out, silu_slope = silu_parts(gate_pre)
    hot_hidden = (hot_weight[:, None] * silu_out * up_pre).astype(jnp.bfloat16)
    hot_out = jnp.dot(hot_hidden, hot_down, preferred_element_type=jnp.float32)
    hot_back = jnp.dot(cotangent, hot_down.T, preferred_element_type=jnp.float32)
    hidden_grad = hot_weight[:, None] * hot_back
    gate_grad = (hidden_grad * up_pre * silu_slope).astype(jnp.bfloat16)
    up_grad = (hidden_grad * silu_out).astype(jnp.bfloat16)
    hot_dx = jnp.dot(gate_grad, hot_in[0], preferred_element_type=jnp.float32) + jnp.dot(up_grad, hot_in[1], preferred_element_type=jnp.float32)
    scale_hot = 1.0 / math.sqrt(TOKENS)
    hot_grad_down = jnp.dot(hot_hidden.T, cotangent, preferred_element_type=jnp.float32) * scale_hot
    hot_grad_in = jnp.stack([jnp.dot(gate_grad.T, tokens, preferred_element_type=jnp.float32), jnp.dot(up_grad.T, tokens, preferred_element_type=jnp.float32)]) * scale_hot
    half_units = FFW // 2
    split_in = cold_in.reshape(2, COLD, 2, half_units, D).astype(jnp.float32)
    split_down = cold_down.reshape(COLD, 2, half_units, D).astype(jnp.float32)
    scale_cold = 1.0 / math.sqrt(N_EXPERT * TOK_DEV)
    places = COLD * N_EXPERT * CAP

    def one_group(pieces):
        group_tok, group_cot, group_ids, group_gate = pieces
        flat_ids = group_ids.reshape(N_EXPERT, TOK_DEV * TOPC)
        one_hot = (flat_ids[:, :, None] == jnp.arange(COLD, dtype=jnp.int32)[None, None, :]).astype(jnp.int32)
        earlier = jnp.cumsum(one_hot, axis=1) - one_hot
        slot_pos = lax.optimization_barrier(jnp.sum(one_hot * earlier, axis=2))
        target = flat_ids * (N_EXPERT * CAP) + jnp.arange(N_EXPERT, dtype=jnp.int32)[:, None] * CAP + slot_pos
        target = target.reshape(-1).astype(jnp.int32)
        row_tok = jnp.repeat(group_tok, TOPC, axis=1).reshape(-1, D)
        gates_flat = group_gate.reshape(-1)
        row_cot = (gates_flat[:, None] * jnp.repeat(group_cot, TOPC, axis=1).reshape(-1, D)).astype(jnp.bfloat16)
        slots_tok = jnp.zeros((places, D), jnp.bfloat16).at[target].set(row_tok)
        slots_cot = jnp.zeros((places, D), jnp.bfloat16).at[target].set(row_cot)
        xs_wide = slots_tok.reshape(COLD, N_EXPERT * CAP, D).astype(jnp.float32)
        cot_wide = slots_cot.reshape(COLD, N_EXPERT * CAP, D).astype(jnp.float32)
        out_total = jnp.zeros((COLD, N_EXPERT * CAP, D), jnp.float32)
        dx_total = jnp.zeros((COLD, N_EXPERT * CAP, D), jnp.float32)
        grads_in = []
        grads_down = []
        for half in range(2):
            gate_w = split_in[0, :, half]
            up_w = split_in[1, :, half]
            down_w = split_down[:, half]
            cold_gate_pre = jnp.einsum('erd,eud->eru', xs_wide, gate_w)
            cold_up_pre = jnp.einsum('erd,eud->eru', xs_wide, up_w)
            cold_silu, cold_slope = silu_parts(cold_gate_pre)
            cold_hidden = (cold_silu * cold_up_pre).astype(jnp.bfloat16).astype(jnp.float32)
            half_out = jnp.einsum('eru,eud->erd', cold_hidden, down_w).astype(jnp.bfloat16)
            cold_back = jnp.einsum('erd,eud->eru', cot_wide, down_w)
            cold_gate_grad = (cold_back * cold_up_pre * cold_slope).astype(jnp.bfloat16).astype(jnp.float32)
            cold_up_grad = (cold_back * cold_silu).astype(jnp.bfloat16).astype(jnp.float32)
            half_dx = (jnp.einsum('eru,eud->erd', cold_gate_grad, gate_w) + jnp.einsum('eru,eud->erd', cold_up_grad, up_w)).astype(jnp.bfloat16)
            out_total = out_total + half_out.astype(jnp.float32)
            dx_total = dx_total + half_dx.astype(jnp.float32)
            grads_down.append(jnp.einsum('eru,erd->eud', cold_hidden, cot_wide))
            grads_in.append(jnp.stack([jnp.einsum('eru,erd->eud', cold_gate_grad, xs_wide), jnp.einsum('eru,erd->eud', cold_up_grad, xs_wide)]))
        out_rows = out_total.reshape(places, D)[target].reshape(N_EXPERT, TOK_DEV, TOPC, D)
        dx_rows = dx_total.reshape(places, D)[target].reshape(N_EXPERT, TOK_DEV, TOPC, D)
        cold_y = lax.optimization_barrier(jnp.sum(group_gate.reshape(N_EXPERT, TOK_DEV, TOPC, 1) * out_rows, axis=2))
        cold_dx = lax.optimization_barrier(jnp.sum(dx_rows, axis=2))
        grad_down = (jnp.stack(grads_down, axis=1).reshape(COLD * FFW, D) * scale_cold).astype(jnp.bfloat16)
        grad_in = (jnp.stack(grads_in, axis=2).reshape(2, COLD * FFW, D) * scale_cold).astype(jnp.bfloat16)
        return (cold_y, cold_dx, grad_in, grad_down)
    cold_y, cold_dx, cold_grad_in, cold_grad_down = lax.map(one_group, (tokens.reshape(N_DP, N_EXPERT, TOK_DEV, D), cotangent.reshape(N_DP, N_EXPERT, TOK_DEV, D), cold_ids.reshape(N_DP, N_EXPERT, TOK_DEV, TOPC), cold_gate.reshape(N_DP, N_EXPERT, TOK_DEV, TOPC)))
    mixed = (hot_out + cold_y.reshape(TOKENS, D)).astype(jnp.bfloat16)
    input_grad = (hot_dx + cold_dx.reshape(TOKENS, D)).astype(jnp.bfloat16)
    return (mixed, input_grad, hot_grad_in, hot_grad_down, cold_grad_in, cold_grad_down)
```

```python
import math

import jax
import jax.numpy as jnp
from jax import lax
from jax.sharding import PartitionSpec as P


def silu_parts(values):
    sigmoid_val = jax.nn.sigmoid(values)
    return (values * sigmoid_val, sigmoid_val * (1.0 + values * (1.0 - sigmoid_val)))


def hot_terms(tokens, cotangent, hot_weight, weights):
    pre_act = jnp.einsum("td,kud->ktu", tokens, weights[:2], preferred_element_type=jnp.float32)
    silu_out, silu_slope = silu_parts(pre_act[0])
    hidden = (hot_weight[:, None] * silu_out * pre_act[1]).astype(jnp.bfloat16)
    out_part = jnp.dot(hidden, weights[2], preferred_element_type=jnp.float32)
    back_proj = jnp.einsum("td,ud->tu", cotangent, weights[2], preferred_element_type=jnp.float32)
    hidden_grad = hot_weight[:, None] * back_proj
    pre_grad = jnp.stack([hidden_grad * pre_act[1] * silu_slope, hidden_grad * silu_out]).astype(
        jnp.bfloat16
    )
    dx_part = jnp.einsum("ktu,kud->td", pre_grad, weights[:2], preferred_element_type=jnp.float32)
    return (out_part, dx_part, jnp.concatenate([pre_grad, hidden[None]], axis=0))


def cold_terms(row_block, cold_in, cold_down):
    pre_act = jnp.einsum("rd,kud->kru", row_block[0], cold_in, preferred_element_type=jnp.float32)
    silu_out, silu_slope = silu_parts(pre_act[0])
    hidden = (silu_out * pre_act[1]).astype(jnp.bfloat16)
    out_part = jnp.dot(hidden, cold_down, preferred_element_type=jnp.float32).astype(jnp.bfloat16)
    back_proj = jnp.einsum("rd,ud->ru", row_block[1], cold_down, preferred_element_type=jnp.float32)
    pre_grad = jnp.stack([back_proj * pre_act[1] * silu_slope, back_proj * silu_out]).astype(
        jnp.bfloat16
    )
    dx_part = jnp.einsum(
        "kru,kud->rd", pre_grad, cold_in, preferred_element_type=jnp.float32
    ).astype(jnp.bfloat16)
    grad_in = jnp.einsum("kru,rd->kud", pre_grad, row_block[0], preferred_element_type=jnp.float32)
    grad_down = jnp.einsum("ru,rd->ud", hidden, row_block[1], preferred_element_type=jnp.float32)
    return (out_part, dx_part, grad_in, grad_down)


def body(
    tokens, cotangent, hot_mask, hot_gate, cold_ids, cold_gate, hot_in, hot_down, cold_in, cold_down
):
    tok_dev, model_width = tokens.shape
    top_cold = cold_ids.shape[1]
    data_count = lax.axis_size("dp")
    owner_count = lax.axis_size("expert")
    cold_count = owner_count // 2
    capacity = 5 * tok_dev * top_cold // (4 * cold_count)
    hot_weight = hot_mask.astype(jnp.float32) * hot_gate
    hot_stack = jnp.concatenate([hot_in, hot_down[None]], axis=0)
    ids_flat = cold_ids.reshape(-1)
    one_hot = (ids_flat[:, None] == jnp.arange(cold_count, dtype=jnp.int32)[None, :]).astype(
        jnp.int32
    )
    earlier = jnp.cumsum(one_hot, axis=0) - one_hot
    slot_pos = jnp.sum(one_hot * earlier, axis=1)
    column = ids_flat * capacity + slot_pos
    dispatch = (
        column[:, None] == jnp.arange(cold_count * capacity, dtype=jnp.int32)[None, :]
    ).astype(jnp.bfloat16)
    gates_flat = cold_gate.reshape(-1)
    row_tok = jnp.repeat(tokens, top_cold, axis=0)
    row_cot = (gates_flat[:, None] * jnp.repeat(cotangent, top_cold, axis=0)).astype(jnp.bfloat16)
    stacked = jnp.stack([row_tok, row_cot])
    send_rows = jnp.einsum(
        "rc,srd->scd", dispatch, stacked, preferred_element_type=jnp.float32
    ).astype(jnp.bfloat16)
    send_rows = send_rows.reshape(2, cold_count, capacity, model_width)
    duplicate = jnp.broadcast_to(
        send_rows[:, :, None], (2, cold_count, 2, capacity, model_width)
    ).reshape(2, owner_count, capacity, model_width)
    received = lax.all_to_all(duplicate, "expert", split_axis=1, concat_axis=1, tiled=True)
    full_stack = lax.all_gather(hot_stack, "dp", axis=1, tiled=True)
    received, full_stack = lax.optimization_barrier((received, full_stack))
    width = model_width // owner_count
    by_column = jnp.stack([tokens, cotangent]).reshape(2, tok_dev, owner_count, width)
    columns = lax.all_to_all(
        by_column.transpose(0, 2, 1, 3), "expert", split_axis=1, concat_axis=1, tiled=True
    ).reshape(2, owner_count * tok_dev, width)
    row_block = received.reshape(2, owner_count * capacity, model_width)
    out_part, dx_part, cold_grad_in, cold_grad_down = cold_terms(row_block, cold_in, cold_down)
    returned = lax.all_to_all(
        jnp.stack([out_part, dx_part]).reshape(2, owner_count, capacity, model_width),
        "expert",
        split_axis=1,
        concat_axis=1,
        tiled=True,
    )
    pick = jnp.broadcast_to(
        dispatch.reshape(-1, cold_count, 1, capacity), (dispatch.shape[0], cold_count, 2, capacity)
    ).reshape(dispatch.shape[0], owner_count * capacity)
    picked = jnp.einsum(
        "rc,scd->srd",
        pick,
        returned.reshape(2, owner_count * capacity, model_width),
        preferred_element_type=jnp.float32,
    )
    cold_out = jnp.sum(
        gates_flat.reshape(tok_dev, top_cold, 1)
        * picked[0].reshape(tok_dev, top_cold, model_width),
        axis=1,
    )
    cold_dx = jnp.sum(picked[1].reshape(tok_dev, top_cold, model_width), axis=1)
    hot_out, hot_dx, unit_rows = hot_terms(tokens, cotangent, hot_weight, full_stack)
    group_rows = lax.all_gather(unit_rows, "expert", axis=1, tiled=True)
    group_in = jnp.einsum(
        "ktu,td->kud", group_rows[:2], columns[0], preferred_element_type=jnp.float32
    )
    group_down = jnp.einsum(
        "tu,td->ud", group_rows[2], columns[1], preferred_element_type=jnp.float32
    )
    group_grads = jnp.concatenate([group_in, group_down[None]], axis=0)
    scale_hot = 1.0 / math.sqrt(tok_dev * data_count * owner_count)
    hot_cols = lax.psum_scatter(group_grads, "dp", scatter_dimension=1, tiled=True) * scale_hot
    scale_cold = 1.0 / math.sqrt(tok_dev * owner_count)
    mixed = (hot_out + cold_out).astype(jnp.bfloat16)
    input_grad = (hot_dx + cold_dx).astype(jnp.bfloat16)
    return (
        mixed,
        input_grad,
        hot_cols[:2],
        hot_cols[2],
        (cold_grad_in * scale_cold).astype(jnp.bfloat16)[None],
        (cold_grad_down * scale_cold).astype(jnp.bfloat16)[None],
    )


def solution(mesh):
    return jax.shard_map(
        body,
        mesh=mesh,
        in_specs=(
            P(("dp", "expert"), None),
            P(("dp", "expert"), None),
            P(("dp", "expert")),
            P(("dp", "expert")),
            P(("dp", "expert"), None),
            P(("dp", "expert"), None),
            P(None, "dp", None),
            P("dp", None),
            P(None, "expert", None),
            P("expert", None),
        ),
        out_specs=(
            P(("dp", "expert"), None),
            P(("dp", "expert"), None),
            P(None, "dp", "expert"),
            P("dp", "expert"),
            P("dp", None, "expert", None),
            P("dp", "expert", None),
        ),
        check_vma=False,
    )
```
